512 devices in a mesh: inner: 32 (over y, x, core), outer: 16 (over z).
Axes of the slice: x: 4, y: 4, z: 16, core: 2. Of those that a mesh axis runs over, the one named last changes fastest.
Arguments:
- activations: bfloat16 [131072, 8192], P(('inner', 'outer')), may hold values from -24 to 24
- output_grads: bfloat16 [131072, 512], P(('inner', 'outer')), may hold values from -0.015625 to 0.015625
Outputs:
- weight_grad: float32 [8192, 512], P(('inner', 'outer'))
The draws below stay inside these ranges and needn't reach their ends.
All inputs are finite; a program needn't handle non-finite values.
Results may differ from the reference program's by a relative error of at most 0.0055.
The reference program's roundings to bfloat16 on the way count: a program that leaves them out, or rounds other values in their place, can miss the bound.
Values may be sent and summed in bfloat16 or wider, within the bound.
No kernel may reach another device: no remote copies, remote signals or barrier semaphores. Data moves between devices by JAX's collectives and lax.ppermute only.
A program may use at most 192 MiB of HBM per device.

```python
import jax
import jax.numpy as jnp
from jax import lax

D = 8192
COLS = 512
BLOCK = 128
TOK_DEV = 256
TOKENS = 131072
NBLK = 4
N_INNER = 32
N_OUTER = 16


def raised(drawn, own_key, source, target, shards_of, factor):
    def block_of(axis_at):
        return (jnp.arange(drawn.shape[axis_at]) // (drawn.shape[axis_at] // shards_of)).reshape((-1,) + (1,) * (drawn.ndim - 1 - axis_at))

    near = jax.random.permutation(own_key, shards_of)[block_of(target)]
    second = (block_of(target) + shards_of // 2) % shards_of
    return jnp.where((block_of(source) == near) | (block_of(source) == second), factor * drawn, drawn)


def block_levels(own_key, shape, split, least, largest):
    def one(position, parts):
        steps = jax.random.uniform(jax.random.fold_in(jax.random.fold_in(own_key, 6), position), (parts,), jnp.float32, least / len(split), largest / len(split))
        return jnp.repeat(jnp.exp(steps), shape[position] // parts).reshape((-1,) + (1,) * (len(shape) - position - 1))

    level = one(*split[0])
    for cut in split[1:]:
        level = level * one(*cut)
    return level


def gaussian(stream_key, dims, scale, most, shards=(), kind=jnp.bfloat16):
    entries = jax.random.normal(stream_key, dims, jnp.float32) * scale
    if len(shards) > 0:
        entries = block_levels(stream_key, dims, shards, -0.22, 0.18) * entries
    return jnp.clip(entries, min=-most, max=most).astype(kind)


def bell_draw_with(stream_key, dims, spread, bound, cuts, heavy, held_as=jnp.bfloat16):
    result = spread * jax.random.normal(stream_key, dims, jnp.float32)
    if cuts:
        result = result * block_levels(stream_key, dims, cuts, -0.22, 0.18)
    return jnp.clip(raised(result, jax.random.fold_in(stream_key, 3), *heavy), -bound, bound).astype(held_as)


def setup_inputs(seed: int = 0) -> dict:
    arg_keys = jax.random.split(jax.random.key(seed), 3)
    return {
        "activations": bell_draw_with(arg_keys[0], (TOKENS, D), 1.0, 24.0, ((0, 512),), (0, 1, 512, 6.0)),
        "output_grads": gaussian(arg_keys[1], (TOKENS, COLS), TOKENS ** -0.5, 0.015625, ((0, 512),)),
    }


def to_grid(values):
    magnitude = jnp.abs(values)
    spacing = jnp.full_like(values, 2.0 ** -9)
    for power in range(-5, 9):
        spacing = jnp.where(magnitude >= 2.0 ** power, 2.0 ** (power - 3), spacing)
    return jnp.floor(values / spacing + 0.5) * spacing


def quantize(grad):
    blocks = grad.reshape(grad.shape[0], NBLK, BLOCK)
    scale = ((jnp.max(jnp.abs(blocks), axis=-1) + 1e-6) / 448.0).astype(jnp.bfloat16)
    widened = lax.optimization_barrier(scale).astype(jnp.float32)
    codes = to_grid(blocks / widened[..., None]).astype(jnp.bfloat16)
    return codes, scale


def dequantize(codes, scale):
    values = codes.astype(jnp.float32) * scale.astype(jnp.float32)[..., None]
    return values.reshape(values.shape[0], COLS)


def reference(activations, output_grads):
    acts = activations.reshape(N_INNER, N_OUTER, TOK_DEV, D)
    grads = output_grads.reshape(N_INNER, N_OUTER, TOK_DEV, COLS)

    def outer_step(total, outer_idx):
        acts_group = lax.dynamic_index_in_dim(acts, outer_idx, 1, keepdims=False)
        grads_group = lax.dynamic_index_in_dim(grads, outer_idx, 1, keepdims=False)

        def inner_step(acc, pair):
            local = lax.dot_general(pair[0], pair[1], (((0,), (0,)), ((), ())), preferred_element_type=jnp.float32)
            codes, scale = quantize(local)
            return acc + dequantize(codes, scale), None

        group_sum, unused = lax.scan(inner_step, jnp.zeros((D, COLS), jnp.float32), (acts_group, grads_group))
        codes, scale = quantize(group_sum)
        return total + dequantize(codes, scale), None

    total, unused = lax.scan(outer_step, jnp.zeros((D, COLS), jnp.float32), jnp.arange(N_OUTER, dtype=jnp.int32))
    return total
```

```python
import functools
import math

import jax
import jax.numpy as jnp
from jax import lax
from jax.experimental import pallas as pl
from jax.experimental.pallas import tpu as pltpu
from jax.sharding import PartitionSpec as P

BLOCK = 128
COLS = 512
NBLK = COLS // BLOCK
PART = 256
NX = 4
NY = 4
TAIL = 16
F32 = jnp.float32
BF16 = jnp.bfloat16
SPAN = 124.0 * math.log(2.0)


def to_grid(x):
    x = x + jnp.abs(x) * (2.0**-22)
    c = x * (2.0**20 + 1.0)
    fine = c - (c - x)
    coarse = (x + 24576.0) - 24576.0
    return jnp.where(jnp.abs(x) < 2.0**-6, coarse, fine)


def quantize(g):
    top = jnp.max(jnp.abs(g), axis=0, keepdims=True)
    scale = ((top + 1e-06) / 448.0).astype(BF16).astype(F32)
    return to_grid(g * (1.0 / scale)), scale


def encode(s):
    mag = jnp.abs(s)
    top = jnp.max(mag, axis=0, keepdims=True)
    norm = (top * 1.004 + 1e-30).astype(BF16)
    y = jnp.exp(mag * ((2.0 * SPAN) / norm.astype(F32)) - SPAN)
    return jnp.where(s < 0, -y, y).astype(BF16), norm


def decode(code, norm):
    y = code.astype(F32)
    mag = (jnp.log(jnp.abs(y)) + SPAN) * (norm.astype(F32) * (0.5 / SPAN))
    return jnp.where(y < 0, -mag, mag)


def rows_of(b):
    return pl.ds(b * BLOCK, BLOCK)


def pair_block(gto, gtp, ao, ap, b):
    total = None
    for gt, a in ((gto, ao), (gtp, ap)):
        local = jnp.dot(gt[rows_of(b), :], a[...], preferred_element_type=F32)
        codes, scale = quantize(local)
        part = codes * scale
        total = part if total is None else total + part
    return total


def put_coded(out, totals):
    norms = []
    for b, total in enumerate(totals):
        code, norm = encode(total)
        out[rows_of(b), :] = code
        norms.append(norm.astype(F32))
    n = norms[0].shape[1]
    out[COLS : COLS + TAIL, :] = jnp.concatenate(
        norms + [jnp.zeros((TAIL - NBLK, n), F32)], axis=0
    ).astype(BF16)


def get_coded(ref, b):
    return decode(ref[rows_of(b), :], ref[COLS + b : COLS + b + 1, :])


def pair_sent_kernel(tab, gto, gtp, ao, ap, out):
    put_coded(out, [pair_block(gto, gtp, ao, ap, b) for b in range(NBLK)])


def pair_kept_kernel(tab, gto, gtp, ao, ap, out):
    for b in range(NBLK):
        out[rows_of(b), :] = pair_block(gto, gtp, ao, ap, b)


def pair_sum(kept, tab, gto, gtp, a_own, a_par):
    tok = a_own.shape[0]
    whole = pl.BlockSpec((COLS, tok), lambda q, tab: (0, 0))
    part = pl.BlockSpec((tok, PART), lambda q, tab: (0, tab[q]))
    height = COLS if kept else COLS + TAIL
    return pl.pallas_call(
        pair_kept_kernel if kept else pair_sent_kernel,
        grid_spec=pltpu.PrefetchScalarGridSpec(
            num_scalar_prefetch=1,
            grid=(4,),
            in_specs=[whole, whole, part, part],
            out_specs=pl.BlockSpec((height, PART), lambda q, tab: (0, q)),
        ),
        out_shape=jax.ShapeDtypeStruct((height, 4 * PART), F32 if kept else BF16),
        compiler_params=pltpu.CompilerParams(vmem_limit_bytes=48 * 2**20),
        cost_estimate=pl.CostEstimate(
            flops=4 * COLS * tok * 4 * PART, bytes_accessed=3 * 2**20, transcendentals=2**19
        ),
    )(tab, gto, gtp, a_own, a_par)


def level2_kernel(tab, own, r1, r2, r3, out):
    totals = []
    for b in range(NBLK):
        total = own[rows_of(b), :]
        for r in (r1, r2, r3):
            total = total + get_coded(r, b)
        totals.append(total)
    put_coded(out, totals)


def part_specs():
    return [pl.BlockSpec((COLS, PART), lambda i, tab: (0, tab[0]))] + [
        pl.BlockSpec((COLS + TAIL, PART), lambda i, tab: (0, tab[0]))
    ] * 3


def level2_sent(tab, own, got):
    return pl.pallas_call(
        level2_kernel,
        grid_spec=pltpu.PrefetchScalarGridSpec(
            num_scalar_prefetch=1,
            grid=(1,),
            in_specs=part_specs(),
            out_specs=pl.BlockSpec((COLS + TAIL, PART), lambda i, tab: (0, 0)),
        ),
        out_shape=jax.ShapeDtypeStruct((COLS + TAIL, PART), BF16),
        compiler_params=pltpu.CompilerParams(vmem_limit_bytes=48 * 2**20),
    )(tab, own, *got)


def group_kernel(tab, own, r1, r2, r3, s1, s2, s3, out):
    n = own.shape[1]
    n_outer = out.shape[0]
    rows = n // n_outer
    scales = []
    for b in range(NBLK):
        total = own[rows_of(b), :]
        for r in (r1, r2, r3, s1, s2, s3):
            total = total + get_coded(r, b)
        codes, scale = quantize(total)
        scales.append(scale)
        out[:, b * rows : (b + 1) * rows, :] = codes.T.astype(BF16).reshape(n_outer, rows, BLOCK)
    wide = jnp.concatenate(scales + [jnp.zeros((BLOCK - NBLK, n), F32)], axis=0)
    out[:, NBLK * rows :, :] = wide.T.astype(BF16).reshape(n_outer, rows, BLOCK)


def group_codes(tab, own, got, got2, n_outer):
    shape = (n_outer, (NBLK + 1) * (PART // n_outer), BLOCK)
    return pl.pallas_call(
        group_kernel,
        grid_spec=pltpu.PrefetchScalarGridSpec(
            num_scalar_prefetch=1,
            grid=(1,),
            in_specs=part_specs()
            + [pl.BlockSpec((COLS + TAIL, PART), lambda i, tab: (0, 0))] * 3,
            out_specs=pl.BlockSpec(shape, lambda i, tab: (0, 0, 0)),
        ),
        out_shape=jax.ShapeDtypeStruct(shape, BF16),
        compiler_params=pltpu.CompilerParams(vmem_limit_bytes=48 * 2**20),
    )(tab, own, *got, *got2)


def final_kernel(got, out):
    rows = out.shape[0]
    for b in range(NBLK):
        total = jnp.zeros((rows, BLOCK), F32)
        for s in range(got.shape[0]):
            scale = got[s, NBLK * rows :, b : b + 1].astype(F32)
            total = total + got[s, b * rows : (b + 1) * rows, :].astype(F32) * scale
        out[:, b * BLOCK : (b + 1) * BLOCK] = total


def final_sum(got):
    rows = got.shape[1] // (NBLK + 1)
    return pl.pallas_call(
        final_kernel,
        out_shape=jax.ShapeDtypeStruct((rows, COLS), F32),
        compiler_params=pltpu.CompilerParams(vmem_limit_bytes=48 * 2**20),
    )(got)


def index_of(y, x, c):
    return ((y % NY) * NX + x % NX) * 2 + c


def ring(first, k):
    pairs = []
    for y in range(NY):
        for x in range(NX):
            for c in range(2):
                along_x = (c == 0) == first
                to = index_of(y, x + k, c) if along_x else index_of(y + k, x, c)
                pairs.append((index_of(y, x, c), to))
    return pairs


def shards(activations, output_grads):
    me = lax.axis_index("inner")
    n_outer = lax.axis_size("outer")
    c, x, y = me % 2, (me // 2) % NX, me // (2 * NX)
    swap = [(i, i ^ 1) for i in range(2 * NX * NY)]
    g_par = lax.ppermute(output_grads, "inner", swap)
    a_par = lax.ppermute(activations, "inner", swap)
    gto, gtp = output_grads.T, g_par.T

    def column_parts(k):
        q = jnp.arange(4, dtype=jnp.int32)
        return 2 * jnp.where(c == 0, q * NX + (x + k) % NX, ((y + k) % NY) * NX + q) + c

    got = []
    for k in (2, 1, 3):
        coded = pair_sum(False, column_parts(k), gto, gtp, activations, a_par)
        got.append(lax.ppermute(coded, "inner", ring(True, k)))
    own = pair_sum(True, column_parts(0), gto, gtp, activations, a_par)
    base = jnp.where(c == 0, y, x)

    def part_of(k):
        return ((base + k) % 4).astype(jnp.int32).reshape(1)

    got2 = []
    for k in (2, 1, 3):
        coded = level2_sent(part_of(k), own, got)
        got2.append(lax.ppermute(coded, "inner", ring(False, k)))
    packed = group_codes(part_of(0), own, got, got2, n_outer)
    return final_sum(lax.all_to_all(packed, "outer", split_axis=0, concat_axis=0, tiled=True))


def solution(mesh):
    return jax.shard_map(
        shards,
        mesh=mesh,
        in_specs=(P(("inner", "outer"), None), P(("inner", "outer"), None)),
        out_specs=P(("inner", "outer"), None),
        check_vma=False,
    )
```

```python
import functools

import jax
import jax.numpy as jnp
from jax import lax
from jax.experimental import pallas as pl
from jax.experimental.pallas import tpu as pltpu
from jax.sharding import PartitionSpec as P

BLOCK = 128
COLS = 512
NBLK = COLS // BLOCK
PART = 256
NX = 4
NY = 4
TAIL = 16
F32 = jnp.float32
BF16 = jnp.bfloat16
SPAN = 124.0


def to_grid(x):
    return (x + jnp.abs(x) * (2.0**-22)).astype(jnp.float8_e4m3fn).astype(F32)


def quantize(g):
    top = jnp.max(jnp.abs(g), axis=0, keepdims=True)
    scale = ((top + 1e-06) / 448.0).astype(BF16).astype(F32)
    return to_grid(g * (1.0 / scale)), scale


def encode(s):
    top = jnp.max(jnp.abs(s), axis=0, keepdims=True)
    norm = (top * 1.004 + 1e-30).astype(BF16)
    return jnp.exp2(s * (SPAN / norm.astype(F32))).astype(BF16), norm


def decode(code, norm):
    return jnp.log2(code.astype(F32)) * (norm * (1.0 / SPAN))


def rows_of(b):
    return pl.ds(b * BLOCK, BLOCK)


def lanes_of(q):
    return pl.ds(pl.multiple_of(q * PART, PART), PART)


IN_HBM = pl.BlockSpec(memory_space=pltpu.MemorySpace.HBM)
ANY = pl.BlockSpec(memory_space=pl.ANY)
LARGE = pltpu.CompilerParams(vmem_limit_bytes=63 * 2**20 + 2**19)
SMALL = pltpu.CompilerParams(vmem_limit_bytes=24 * 2**20)


def block_sum(g, a, b):
    total = None
    for i in range(g.shape[0]):
        local = lax.dot_general(
            g[i, :, rows_of(b)], a[i], (((0,), (0,)), ((), ())), preferred_element_type=F32
        )
        codes, scale = quantize(local)
        part = codes * scale
        total = part if total is None else total + part
    return total


def put_coded(out, totals):
    norms = []
    for b, total in enumerate(totals):
        code, norm = encode(total)
        out[rows_of(b), :] = code
        norms.append(norm.astype(F32))
    n = norms[0].shape[1]
    out[COLS : COLS + TAIL, :] = jnp.concatenate(
        norms + [jnp.zeros((TAIL - NBLK, n), F32)], axis=0
    ).astype(BF16)


def get_coded(ref, norms, b):
    return decode(ref[rows_of(b), :], norms[b : b + 1, :])


def norms_of(ref):
    return ref[COLS : COLS + TAIL, :].astype(F32)


def position():
    me = lax.axis_index("inner")
    return me // (2 * NX), (me // 2) % NX, me % 2


def part_for(k, q, other=False):
    y, x, c = position()
    c = 1 - c if other else c
    return 2 * jnp.where(c == 0, q * NX + (x + k) % NX, ((y + k) % NY) * NX + q) + c


SWAPPED = (1, 3, 0)


def gather(a, g, buf, in_sem, parts):
    copies = [
        pltpu.make_async_copy(a.at[:, lanes_of(part)], buf.at[:, pl.ds(j * PART, PART)], in_sem.at[j])
        for j, part in enumerate(parts)
    ]
    n = len(parts)
    copies.append(pltpu.make_async_copy(g, buf.at[:, pl.ds(n * PART, COLS)], in_sem.at[n]))
    return copies


def swap_kernel(a, g, out, buf, in_sem, out_sem):
    copies = gather(a, g, buf, in_sem, [part_for(k, q, True) for k in SWAPPED for q in range(4)])
    for copy in copies:
        copy.start()
    for copy in copies:
        copy.wait()
    put = pltpu.make_async_copy(buf, out, out_sem)
    put.start()
    put.wait()


def swap_payload(a, g):
    shape = (a.shape[0], 12 * PART + COLS)
    return pl.pallas_call(
        swap_kernel,
        in_specs=[IN_HBM, ANY],
        out_specs=ANY,
        scratch_shapes=[
            pltpu.VMEM(shape, BF16),
            pltpu.SemaphoreType.DMA((13,)),
            pltpu.SemaphoreType.DMA,
        ],
        out_shape=jax.ShapeDtypeStruct(shape, BF16),
        compiler_params=LARGE,
    )(a, g)


def far_kernel(a, g, after, same, cross, buf, in_sem, out_sem):
    copies = [
        gather(a, g, buf.at[i], in_sem.at[i], [part_for(2, q, i == 1) for q in range(4)]) for i in range(2)
    ]
    puts = [pltpu.make_async_copy(buf.at[i], (same, cross)[i], out_sem.at[i]) for i in range(2)]
    for i in range(2):
        for copy in copies[i]:
            copy.start()
    for i in range(2):
        for copy in copies[i]:
            copy.wait()
        puts[i].start()
    for put in puts:
        put.wait()


def far_payloads(a, g, after):
    shape = (a.shape[0], 4 * PART + COLS)
    return pl.pallas_call(
        far_kernel,
        in_specs=[IN_HBM, ANY, ANY],
        out_specs=[ANY, ANY],
        scratch_shapes=[
            pltpu.VMEM((2,) + shape, BF16),
            pltpu.SemaphoreType.DMA((2, 5)),
            pltpu.SemaphoreType.DMA((2,)),
        ],
        out_shape=[jax.ShapeDtypeStruct(shape, BF16)] * 2,
        compiler_params=LARGE,
    )(a, g, after)


def sums_kernel(ks, kept, g_own, a_own, swapped, *rest):
    n, far = len(ks), rest[: 2 * kept]
    outs, (gbuf, abuf, obuf, gsem, asem, osem) = rest[2 * kept : 2 * kept + n], rest[2 * kept + n :]
    devices = 2 + len(far)

    def g_in(i):
        if i == 0:
            src = g_own
        else:
            src = swapped.at[:, 12 * PART :] if i == 1 else far[i - 2].at[:, 4 * PART :]
        return pltpu.make_async_copy(src, gbuf.at[i], gsem.at[i])

    def a_in(m, q, i):
        if i == 0:
            src = a_own.at[:, lanes_of(part_for(ks[m], q))]
        elif i == 1:
            src = swapped.at[:, lanes_of(4 * SWAPPED.index(ks[m]) + q)]
        else:
            src = far[i - 2].at[:, lanes_of(q)]
        return pltpu.make_async_copy(src, abuf.at[4 * m + q, i], asem.at[4 * m + q, i])

    def put(m, q):
        return pltpu.make_async_copy(obuf.at[4 * m + q], outs[m].at[:, lanes_of(q)], osem.at[4 * m + q])

    for i in range(devices):
        g_in(i).start()
        a_in(0, 0, i).start()
    for j in range(1, 4 * n):
        for i in range(devices):
            a_in(j // 4, j % 4, i).start()
    for i in range(devices):
        g_in(i).wait()
    for m in range(n):

        def step(q, carry):
            j = 4 * m + q
            for i in range(devices):
                a_in(m, q, i).wait()
            if kept:
                for b in range(NBLK):
                    obuf[j, rows_of(b), :] = block_sum(gbuf, abuf.at[j], b)
            else:
                put_coded(obuf.at[j], [block_sum(gbuf, abuf.at[j], b) for b in range(NBLK)])
            put(m, q).start()
            return carry

        lax.fori_loop(0, 4, step, 0)
    for m in range(n):
        for q in range(4):
            put(m, q).wait()


def sums(ks, g_own, a_own, swapped, far=()):
    n, tok, kept = len(ks), a_own.shape[0], len(far) > 0
    devices = 2 + len(far)
    height, dtype = (COLS, F32) if kept else (COLS + TAIL, BF16)
    return pl.pallas_call(
        functools.partial(sums_kernel, ks, kept),
        in_specs=[ANY, IN_HBM, ANY] + [ANY] * len(far),
        out_specs=[ANY] * n,
        scratch_shapes=[
            pltpu.VMEM((devices, tok, COLS), BF16),
            pltpu.VMEM((4 * n, devices, tok, PART), BF16),
            pltpu.VMEM((4 * n, height, PART), dtype),
            pltpu.SemaphoreType.DMA((devices,)),
            pltpu.SemaphoreType.DMA((4 * n, devices)),
            pltpu.SemaphoreType.DMA((4 * n,)),
        ],
        out_shape=[jax.ShapeDtypeStruct((height, 4 * PART), dtype)] * n,
        compiler_params=LARGE,
        cost_estimate=pl.CostEstimate(
            flops=2 ** (36 if kept else 31), bytes_accessed=2**20, transcendentals=0
        ),
    )(g_own, a_own, swapped, *far)


def row_sum_kernel(own, r0, r1, out, fbuf, rbuf, obuf, fsem, rsem, osem):
    def f_in(q):
        return pltpu.make_async_copy(own.at[:, lanes_of(q)], fbuf.at[q], fsem.at[q])

    def r_in(q, i):
        return pltpu.make_async_copy((r0, r1)[i].at[:, lanes_of(q)], rbuf.at[q, i], rsem.at[q, i])

    def put(q):
        return pltpu.make_async_copy(obuf.at[q], out.at[q], osem.at[q])

    for q in range(4):
        f_in(q).start()
        for i in range(2):
            r_in(q, i).start()

    def step(q, carry):
        f_in(q).wait()
        for i in range(2):
            r_in(q, i).wait()
        norms = [norms_of(rbuf.at[q, i]) for i in range(2)]
        totals = []
        for b in range(NBLK):
            total = fbuf[q, rows_of(b), :]
            for i in range(2):
                total = total + get_coded(rbuf.at[q, i], norms[i], b)
            totals.append(total)
        put_coded(obuf.at[q], totals)
        put(q).start()
        return carry

    lax.fori_loop(0, 4, step, 0)
    for q in range(4):
        put(q).wait()


def row_sum(own, r0, r1):
    return pl.pallas_call(
        row_sum_kernel,
        in_specs=[ANY] * 3,
        out_specs=ANY,
        out_shape=jax.ShapeDtypeStruct((4, COLS + TAIL, PART), BF16),
        scratch_shapes=[
            pltpu.VMEM((4, COLS, PART), F32),
            pltpu.VMEM((4, 2, COLS + TAIL, PART), BF16),
            pltpu.VMEM((4, COLS + TAIL, PART), BF16),
            pltpu.SemaphoreType.DMA((4,)),
            pltpu.SemaphoreType.DMA((4, 2)),
            pltpu.SemaphoreType.DMA((4,)),
        ],
        compiler_params=LARGE,
    )(own, r0, r1)


def group_kernel(got, out):
    n = got.shape[2]
    n_outer = out.shape[0]
    rows = n // n_outer
    norms = [norms_of(got.at[s]) for s in range(4)]
    for b in range(NBLK):
        total = get_coded(got.at[0], norms[0], b)
        for s in range(1, 4):
            total = total + get_coded(got.at[s], norms[s], b)
        codes, scale = quantize(total)
        sent = (codes * scale).T.astype(BF16)
        out[:, b * rows : (b + 1) * rows, :] = sent.reshape(n_outer, rows, BLOCK)


def group_sent(got, n_outer):
    return pl.pallas_call(
        group_kernel,
        out_shape=jax.ShapeDtypeStruct((n_outer, NBLK * (PART // n_outer), BLOCK), BF16),
        compiler_params=SMALL,
    )(got)


def final_kernel(got, out):
    rows = out.shape[0]
    for b in range(NBLK):
        total = jnp.zeros((rows, BLOCK), F32)
        for s in range(got.shape[0]):
            total = total + got[s, b * rows : (b + 1) * rows, :].astype(F32)
        out[:, b * BLOCK : (b + 1) * BLOCK] = total


def final_sum(got):
    rows = got.shape[1] // NBLK
    return pl.pallas_call(
        final_kernel,
        out_shape=jax.ShapeDtypeStruct((rows, COLS), F32),
        compiler_params=SMALL,
    )(got)


def index_of(y, x, c):
    return ((y % NY) * NX + x % NX) * 2 + c


def ring(k, cross=False):
    pairs = []
    for y in range(NY):
        for x in range(NX):
            pairs.append((index_of(y, x, int(cross)), index_of(y, x + k, 0)))
            pairs.append((index_of(y, x, 1 - int(cross)), index_of(y + k, x, 1)))
    return pairs


def columns():
    return [[index_of(y, x, 0) for y in range(NY)] for x in range(NX)] + [
        [index_of(y, x, 1) for x in range(NX)] for y in range(NY)
    ]


def shards(activations, output_grads):
    n_outer = lax.axis_size("outer")
    swap = [(i, i ^ 1) for i in range(2 * NX * NY)]
    to_swap = swap_payload(activations, output_grads)
    swapped = lax.ppermute(to_swap, "inner", swap)
    same, cross = far_payloads(activations, output_grads, to_swap)
    far = (lax.ppermute(same, "inner", ring(2)), lax.ppermute(cross, "inner", ring(2, cross=True)))
    ahead, behind = sums((1, 3), output_grads, activations, swapped)
    got_ahead = lax.ppermute(ahead, "inner", ring(1))
    got_behind = lax.ppermute(behind, "inner", ring(3))
    (own,) = sums((0,), output_grads, activations, swapped, far)
    coded = row_sum(own, got_ahead, got_behind)
    got = lax.all_to_all(
        coded, "inner", split_axis=0, concat_axis=0, tiled=True, axis_index_groups=columns()
    )
    packed = group_sent(got, n_outer)
    return final_sum(lax.all_to_all(packed, "outer", split_axis=0, concat_axis=0, tiled=True))


def solution(mesh):
    return jax.shard_map(
        shards,
        mesh=mesh,
        in_specs=(P(("inner", "outer"), None), P(("inner", "outer"), None)),
        out_specs=P(("inner", "outer"), None),
        check_vma=False,
    )
```

```python
import functools

import jax
import jax.numpy as jnp
from jax import lax
from jax.experimental import pallas as pl
from jax.experimental.pallas import tpu as pltpu
from jax.sharding import PartitionSpec as P

BLOCK = 128
COLS = 512
NBLK = COLS // BLOCK
PART = 256
NX = 4
NY = 4
TAIL = 16
F32 = jnp.float32
BF16 = jnp.bfloat16
SPAN = 124.0


def to_grid(x):
    return (x + jnp.abs(x) * (2.0**-22)).astype(jnp.float8_e4m3fn).astype(F32)


def quantize(g):
    top = jnp.max(jnp.abs(g), axis=0, keepdims=True)
    scale = ((top + 1e-06) / 448.0).astype(BF16).astype(F32)
    return to_grid(g * (1.0 / scale)), scale


def encode(s):
    top = jnp.max(jnp.abs(s), axis=0, keepdims=True)
    norm = (top * 1.004 + 1e-30).astype(BF16)
    return jnp.exp2(s * (SPAN / norm.astype(F32))).astype(BF16), norm


def decode(code, norm):
    return jnp.log2(code.astype(F32)) * (norm * (1.0 / SPAN))


def rows_of(b):
    return pl.ds(b * BLOCK, BLOCK)


def lanes_of(q):
    return pl.ds(pl.multiple_of(q * PART, PART), PART)


HBM, VMEM = pltpu.MemorySpace.HBM, pltpu.MemorySpace.VMEM
ANY, WHOLE = pl.BlockSpec(memory_space=pl.ANY), pl.BlockSpec(memory_space=VMEM)
PARAMS = pltpu.CompilerParams(vmem_limit_bytes=24 * 2**20)


def near(*arrays):
    return [pltpu.with_memory_space_constraint(x, VMEM) for x in arrays]


def block_sum(local, b):
    total = None
    for i in range(local.shape[0]):
        codes, scale = quantize(local[i, rows_of(b), :])
        part = codes * scale
        total = part if total is None else total + part
    return total


def put_coded(out, lanes, totals):
    norms = []
    for b, total in enumerate(totals):
        code, norm = encode(total)
        out[rows_of(b), lanes] = code
        norms.append(norm.astype(F32))
    n = norms[0].shape[1]
    out[COLS : COLS + TAIL, lanes] = jnp.concatenate(
        norms + [jnp.zeros((TAIL - NBLK, n), F32)], axis=0
    ).astype(BF16)


def norms_of(ref, lanes):
    return ref[COLS : COLS + TAIL, lanes].astype(F32)


def get_coded(ref, lanes, norms, b):
    return decode(ref[rows_of(b), lanes], norms[b : b + 1, :])


def position():
    me = lax.axis_index("inner")
    return me // (2 * NX), (me // 2) % NX, me % 2


def part_for(k, q, other=False):
    y, x, c = position()
    c = 1 - c if other else c
    return 2 * jnp.where(c == 0, q * NX + (x + k) % NX, ((y + k) % NY) * NX + q) + c


SWAPPED = (1, 3, 0)


def send_kernel(a, g, *rest):
    outs, sems = rest[:3], rest[3:]
    parts = [
        [part_for(k, q, True) for k in SWAPPED for q in range(4)],
        [part_for(2, q) for q in range(4)],
        [part_for(2, q, True) for q in range(4)],
    ]
    copies = []
    for out, sem, group in zip(outs, sems, parts):
        n = len(group)
        for j, p in enumerate(group):
            copies.append(
                pltpu.make_async_copy(a.at[:, lanes_of(p)], out.at[:, pl.ds(j * PART, PART)], sem.at[j])
            )
        copies.append(pltpu.make_async_copy(g, out.at[:, pl.ds(n * PART, COLS)], sem.at[n]))
    for copy in copies:
        copy.start()
    for copy in copies:
        copy.wait()


def to_send(a, g):
    tok = a.shape[0]
    shapes = [(tok, 12 * PART + COLS)] + [(tok, 4 * PART + COLS)] * 2
    return pl.pallas_call(
        send_kernel,
        in_specs=[ANY, ANY],
        out_specs=[WHOLE] * 3,
        scratch_shapes=[pltpu.SemaphoreType.DMA((n,)) for n in (13, 5, 5)],
        out_shape=[pltpu.VMEM(shape, BF16) for shape in shapes],
        compiler_params=PARAMS,
    )(*[pltpu.with_memory_space_constraint(x, HBM) for x in (a, g)])


def sums_kernel(ks, kept, g_own, a_own, swapped, *rest):
    n = len(ks)
    far, outs, (abuf, gt, local, asem) = rest[: 2 * kept], rest[2 * kept : 2 * kept + n], rest[2 * kept + n :]
    devices = 2 + len(far)

    def a_in(m, q):
        src = a_own.at[:, lanes_of(part_for(ks[m], q))]
        return pltpu.make_async_copy(src, abuf.at[4 * m + q], asem.at[4 * m + q])

    for j in range(4 * n):
        a_in(j // 4, j % 4).start()
    gt[0] = g_own[...].T
    gt[1] = swapped[:, 12 * PART :].T
    for i, other in enumerate(far):
        gt[2 + i] = other[:, 4 * PART :].T
    for m in range(n):

        def step(q, carry):
            lanes = lanes_of(q)
            a_in(m, q).wait()
            columns = [abuf[4 * m + q], swapped[:, lanes_of(4 * SWAPPED.index(ks[m]) + q)]]
            columns += [other[:, lanes] for other in far]
            for i in range(devices):
                local[i] = jnp.dot(gt[i], columns[i], preferred_element_type=F32)
            if kept:
                for b in range(NBLK):
                    outs[0][rows_of(b), lanes] = block_sum(local, b)
            else:
                put_coded(outs[m], lanes, [block_sum(local, b) for b in range(NBLK)])
            return carry

        lax.fori_loop(0, 4, step, 0)


def sums(ks, g_own, a_own, swapped, far=()):
    n, tok, kept = len(ks), a_own.shape[0], len(far) > 0
    devices = 2 + len(far)
    height, dtype = (COLS, F32) if kept else (COLS + TAIL, BF16)
    return pl.pallas_call(
        functools.partial(sums_kernel, ks, kept),
        in_specs=[WHOLE, ANY, WHOLE] + [WHOLE] * len(far),
        out_specs=[WHOLE] * n,
        scratch_shapes=[
            pltpu.VMEM((4 * n, tok, PART), BF16),
            pltpu.VMEM((devices, COLS, tok), BF16),
            pltpu.VMEM((devices, COLS, PART), F32),
            pltpu.SemaphoreType.DMA((4 * n,)),
        ],
        out_shape=[pltpu.VMEM((height, 4 * PART), dtype)] * n,
        compiler_params=PARAMS,
        cost_estimate=pl.CostEstimate(
            flops=2 ** (36 if kept else 31), bytes_accessed=2**20, transcendentals=0
        ),
    )(*near(g_own), pltpu.with_memory_space_constraint(a_own, HBM), *near(swapped, *far))


def row_sum_kernel(own, r0, r1, out):
    def step(q, carry):
        lanes = lanes_of(q)
        norms = [norms_of(r, lanes) for r in (r0, r1)]
        totals = []
        for b in range(NBLK):
            total = own[rows_of(b), lanes]
            for i, r in enumerate((r0, r1)):
                total = total + get_coded(r, lanes, norms[i], b)
            totals.append(total)
        put_coded(out.at[q], slice(None), totals)
        return carry

    lax.fori_loop(0, 4, step, 0)


def row_sum(own, r0, r1):
    return pl.pallas_call(
        row_sum_kernel,
        in_specs=[WHOLE] * 3,
        out_specs=WHOLE,
        out_shape=pltpu.VMEM((4, COLS + TAIL, PART), BF16),
        compiler_params=PARAMS,
    )(*near(own, r0, r1))


def group_kernel(got, out):
    n = got.shape[2]
    n_outer = out.shape[0]
    rows = n // n_outer
    lanes = slice(None)
    norms = [norms_of(got.at[s], lanes) for s in range(4)]
    for b in range(NBLK):
        total = get_coded(got.at[0], lanes, norms[0], b)
        for s in range(1, 4):
            total = total + get_coded(got.at[s], lanes, norms[s], b)
        codes, scale = quantize(total)
        sent = (codes * scale).T.astype(BF16)
        out[:, b * rows : (b + 1) * rows, :] = sent.reshape(n_outer, rows, BLOCK)


def group_sent(got, n_outer):
    return pl.pallas_call(
        group_kernel,
        in_specs=[WHOLE],
        out_specs=WHOLE,
        out_shape=pltpu.VMEM((n_outer, NBLK * (PART // n_outer), BLOCK), BF16),
        compiler_params=PARAMS,
    )(*near(got))


def final_kernel(got, out):
    rows = out.shape[0]
    for b in range(NBLK):
        total = jnp.zeros((rows, BLOCK), F32)
        for s in range(got.shape[0]):
            total = total + got[s, b * rows : (b + 1) * rows, :].astype(F32)
        out[:, b * BLOCK : (b + 1) * BLOCK] = total


def final_sum(got):
    rows = got.shape[1] // NBLK
    return pl.pallas_call(
        final_kernel,
        out_shape=jax.ShapeDtypeStruct((rows, COLS), F32),
        compiler_params=PARAMS,
    )(*near(got))


def index_of(y, x, c):
    return ((y % NY) * NX + x % NX) * 2 + c


def ring(k, cross=False):
    pairs = []
    for y in range(NY):
        for x in range(NX):
            pairs.append((index_of(y, x, int(cross)), index_of(y, x + k, 0)))
            pairs.append((index_of(y, x, 1 - int(cross)), index_of(y + k, x, 1)))
    return pairs


def columns():
    return [[index_of(y, x, 0) for y in range(NY)] for x in range(NX)] + [
        [index_of(y, x, 1) for x in range(NX)] for y in range(NY)
    ]


def shards(activations, output_grads):
    n_outer = lax.axis_size("outer")
    swap = [(i, i ^ 1) for i in range(2 * NX * NY)]
    to_swap, same, cross = to_send(activations, output_grads)
    swapped = lax.ppermute(to_swap, "inner", swap)
    far = (lax.ppermute(same, "inner", ring(2)), lax.ppermute(cross, "inner", ring(2, cross=True)))
    ahead, behind = sums((1, 3), output_grads, activations, swapped)
    got_ahead = lax.ppermute(ahead, "inner", ring(1))
    got_behind = lax.ppermute(behind, "inner", ring(3))
    (own,) = sums((0,), output_grads, activations, swapped, far)
    coded = row_sum(own, got_ahead, got_behind)
    got = lax.all_to_all(
        coded, "inner", split_axis=0, concat_axis=0, tiled=True, axis_index_groups=columns()
    )
    packed = group_sent(got, n_outer)
    return final_sum(lax.all_to_all(packed, "outer", split_axis=0, concat_axis=0, tiled=True))


def solution(mesh):
    return jax.shard_map(
        shards,
        mesh=mesh,
        in_specs=(P(("inner", "outer"), None), P(("inner", "outer"), None)),
        out_specs=P(("inner", "outer"), None),
        check_vma=False,
    )
```

```python
import functools

import jax
import jax.numpy as jnp
from jax import lax
from jax.experimental import pallas as pl
from jax.experimental.pallas import tpu as pltpu
from jax.sharding import PartitionSpec as P

BLOCK = 128
COLS = 512
NBLK = COLS // BLOCK
PART = 256
NX = 4
NY = 4
TAIL = 16
F32 = jnp.float32
BF16 = jnp.bfloat16
SPAN = 124.0


def to_grid(x):
    return (x + jnp.abs(x) * (2.0**-22)).astype(jnp.float8_e4m3fn).astype(F32)


def quantize(g):
    top = jnp.max(jnp.abs(g), axis=0, keepdims=True)
    scale = ((top + 1e-06) / 448.0).astype(BF16).astype(F32)
    return to_grid(g * (1.0 / scale)), scale


def encode(s):
    top = jnp.max(jnp.abs(s), axis=0, keepdims=True)
    norm = (top * 1.004 + 1e-30).astype(BF16)
    return jnp.exp2(s * (SPAN / norm.astype(F32))).astype(BF16), norm


def decode(code, norm):
    return jnp.log2(code.astype(F32)) * (norm * (1.0 / SPAN))


def rows_of(b):
    return pl.ds(b * BLOCK, BLOCK)


def lanes_of(q):
    return pl.ds(pl.multiple_of(q * PART, PART), PART)


HBM, VMEM = pltpu.MemorySpace.HBM, pltpu.MemorySpace.VMEM
ANY, WHOLE = pl.BlockSpec(memory_space=pl.ANY), pl.BlockSpec(memory_space=VMEM)
PARAMS = pltpu.CompilerParams(vmem_limit_bytes=24 * 2**20)


def near(*arrays):
    return [pltpu.with_memory_space_constraint(x, VMEM) for x in arrays]


def block_sum(local, b):
    total = None
    for i in range(local.shape[0]):
        codes, scale = quantize(local[i, rows_of(b), :])
        part = codes * scale
        total = part if total is None else total + part
    return total


def put_coded(out, lanes, totals):
    norms = []
    for b, total in enumerate(totals):
        code, norm = encode(total)
        out[rows_of(b), lanes] = code
        norms.append(norm.astype(F32))
    n = norms[0].shape[1]
    out[COLS : COLS + TAIL, lanes] = jnp.concatenate(
        norms + [jnp.zeros((TAIL - NBLK, n), F32)], axis=0
    ).astype(BF16)


def norms_of(ref, lanes):
    return ref[COLS : COLS + TAIL, lanes].astype(F32)


def get_coded(ref, lanes, norms, b):
    return decode(ref[rows_of(b), lanes], norms[b : b + 1, :])


def position():
    me = lax.axis_index("inner")
    return me // (2 * NX), (me // 2) % NX, me % 2


def part_for(k, q, other=False):
    y, x, c = position()
    c = 1 - c if other else c
    return 2 * jnp.where(c == 0, q * NX + (x + k) % NX, ((y + k) % NY) * NX + q) + c


SWAPPED = (1, 3, 0)


def send_kernel(a, g, *rest):
    outs, sems = rest[:3], rest[3:]
    parts = [
        [part_for(k, q, True) for k in SWAPPED for q in range(4)],
        [part_for(2, q) for q in range(4)],
        [part_for(2, q, True) for q in range(4)],
    ]
    copies = []
    for out, sem, group in zip(outs, sems, parts):
        n = len(group)
        for j, p in enumerate(group):
            copies.append(
                pltpu.make_async_copy(a.at[:, lanes_of(p)], out.at[:, pl.ds(j * PART, PART)], sem.at[j])
            )
        copies.append(pltpu.make_async_copy(g, out.at[:, pl.ds(n * PART, COLS)], sem.at[n]))
    for copy in copies:
        copy.start()
    for copy in copies:
        copy.wait()


def to_send(a, g):
    tok = a.shape[0]
    shapes = [(tok, 12 * PART + COLS)] + [(tok, 4 * PART + COLS)] * 2
    return pl.pallas_call(
        send_kernel,
        in_specs=[ANY, ANY],
        out_specs=[WHOLE] * 3,
        scratch_shapes=[pltpu.SemaphoreType.DMA((n,)) for n in (13, 5, 5)],
        out_shape=[pltpu.VMEM(shape, BF16) for shape in shapes],
        compiler_params=PARAMS,
    )(*[pltpu.with_memory_space_constraint(x, HBM) for x in (a, g)])


def sums_kernel(ks, kept, g_own, a_own, swapped, *rest):
    n = len(ks)
    far, outs, (abuf, gt, local, asem) = rest[: 2 * kept], rest[2 * kept : 2 * kept + n], rest[2 * kept + n :]
    devices = 2 + len(far)

    def a_in(m, q):
        src = a_own.at[:, lanes_of(part_for(ks[m], q))]
        return pltpu.make_async_copy(src, abuf.at[4 * m + q], asem.at[4 * m + q])

    for j in range(4 * n):
        a_in(j // 4, j % 4).start()
    gt[0] = g_own[...].T
    gt[1] = swapped[:, 12 * PART :].T
    for i, other in enumerate(far):
        gt[2 + i] = other[:, 4 * PART :].T
    for m in range(n):

        def step(q, carry):
            lanes = lanes_of(q)
            a_in(m, q).wait()
            columns = [abuf[4 * m + q], swapped[:, lanes_of(4 * SWAPPED.index(ks[m]) + q)]]
            columns += [other[:, lanes] for other in far]
            for i in range(devices):
                local[i] = jnp.dot(gt[i], columns[i], preferred_element_type=F32)
            if kept:
                for b in range(NBLK):
                    outs[0][rows_of(b), lanes] = block_sum(local, b)
            else:
                put_coded(outs[m], lanes, [block_sum(local, b) for b in range(NBLK)])
            return carry

        lax.fori_loop(0, 4, step, 0)


def sums(ks, g_own, a_own, swapped, far=()):
    n, tok, kept = len(ks), a_own.shape[0], len(far) > 0
    devices = 2 + len(far)
    height, dtype = (COLS, F32) if kept else (COLS + TAIL, BF16)
    return pl.pallas_call(
        functools.partial(sums_kernel, ks, kept),
        in_specs=[WHOLE, ANY, WHOLE] + [WHOLE] * len(far),
        out_specs=[WHOLE] * n,
        scratch_shapes=[
            pltpu.VMEM((4 * n, tok, PART), BF16),
            pltpu.VMEM((devices, COLS, tok), BF16),
            pltpu.VMEM((devices, COLS, PART), F32),
            pltpu.SemaphoreType.DMA((4 * n,)),
        ],
        out_shape=[pltpu.VMEM((height, 4 * PART), dtype)] * n,
        compiler_params=PARAMS,
        cost_estimate=pl.CostEstimate(
            flops=2 ** (36 if kept else 31), bytes_accessed=2**20, transcendentals=0
        ),
    )(*near(g_own), pltpu.with_memory_space_constraint(a_own, HBM), *near(swapped, *far))


def row_sum_kernel(own, r0, r1, out):
    def step(q, carry):
        lanes = lanes_of(q)
        norms = [norms_of(r, lanes) for r in (r0, r1)]
        totals = []
        for b in range(NBLK):
            total = own[rows_of(b), lanes]
            for i, r in enumerate((r0, r1)):
                total = total + get_coded(r, lanes, norms[i], b)
            totals.append(total)
        put_coded(out.at[q], slice(None), totals)
        return carry

    lax.fori_loop(0, 4, step, 0)


def row_sum(own, r0, r1):
    return pl.pallas_call(
        row_sum_kernel,
        in_specs=[WHOLE] * 3,
        out_specs=WHOLE,
        out_shape=pltpu.VMEM((4, COLS + TAIL, PART), BF16),
        compiler_params=PARAMS,
    )(*near(own, r0, r1))


def group_kernel(got, out):
    n = got.shape[2]
    n_outer = out.shape[0]
    rows = n // n_outer
    lanes = slice(None)
    norms = [norms_of(got.at[s], lanes) for s in range(4)]
    for b in range(NBLK):
        total = get_coded(got.at[0], lanes, norms[0], b)
        for s in range(1, 4):
            total = total + get_coded(got.at[s], lanes, norms[s], b)
        codes, scale = quantize(total)
        sent = (codes * scale).T.astype(BF16)
        out[:, b * rows : (b + 1) * rows, :] = sent.reshape(n_outer, rows, BLOCK)


def group_sent(got, n_outer):
    return pl.pallas_call(
        group_kernel,
        in_specs=[WHOLE],
        out_specs=WHOLE,
        out_shape=pltpu.VMEM((n_outer, NBLK * (PART // n_outer), BLOCK), BF16),
        compiler_params=PARAMS,
    )(*near(got))


def final_kernel(got, out):
    rows = out.shape[0]
    for b in range(NBLK):
        total = jnp.zeros((rows, BLOCK), F32)
        for s in range(got.shape[0]):
            total = total + got[s, b * rows : (b + 1) * rows, :].astype(F32)
        out[:, b * BLOCK : (b + 1) * BLOCK] = total


def final_sum(got):
    rows = got.shape[1] // NBLK
    return pl.pallas_call(
        final_kernel,
        out_shape=jax.ShapeDtypeStruct((rows, COLS), F32),
        compiler_params=PARAMS,
    )(*near(got))


def index_of(y, x, c):
    return ((y % NY) * NX + x % NX) * 2 + c


def ring(k, cross=False):
    pairs = []
    for y in range(NY):
        for x in range(NX):
            pairs.append((index_of(y, x, int(cross)), index_of(y, x + k, 0)))
            pairs.append((index_of(y, x, 1 - int(cross)), index_of(y + k, x, 1)))
    return pairs


def columns():
    return [[index_of(y, x, 0) for y in range(NY)] for x in range(NX)] + [
        [index_of(y, x, 1) for x in range(NX)] for y in range(NY)
    ]


def shards(activations, output_grads):
    n_outer = lax.axis_size("outer")
    swap = [(i, i ^ 1) for i in range(2 * NX * NY)]
    to_swap, same, cross = to_send(activations, output_grads)
    got_same = lax.ppermute(same, "inner", ring(2))
    swapped = lax.ppermute(to_swap, "inner", swap)
    far = (got_same, lax.ppermute(cross, "inner", ring(2, cross=True)))
    (ahead,) = sums((1,), output_grads, activations, swapped)
    got_ahead = lax.ppermute(ahead, "inner", ring(1))
    (behind,) = sums((3,), output_grads, activations, swapped)
    got_behind = lax.ppermute(behind, "inner", ring(3))
    (own,) = sums((0,), output_grads, activations, swapped, far)
    coded = row_sum(own, got_ahead, got_behind)
    got = lax.all_to_all(
        coded, "inner", split_axis=0, concat_axis=0, tiled=True, axis_index_groups=columns()
    )
    packed = group_sent(got, n_outer)
    return final_sum(lax.all_to_all(packed, "outer", split_axis=0, concat_axis=0, tiled=True))


def solution(mesh):
    return jax.shard_map(
        shards,
        mesh=mesh,
        in_specs=(P(("inner", "outer"), None), P(("inner", "outer"), None)),
        out_specs=P(("inner", "outer"), None),
        check_vma=False,
    )
```

```python
import functools

import jax
import jax.numpy as jnp
from jax import lax
from jax.experimental import pallas as pl
from jax.experimental.pallas import tpu as pltpu
from jax.sharding import PartitionSpec as P

BLOCK = 128
COLS = 512
NBLK = COLS // BLOCK
PART = 256
NX = 4
NY = 4
TAIL = 16
F32 = jnp.float32
BF16 = jnp.bfloat16
SPAN = 124.0


def to_grid(x):
    return (x + jnp.abs(x) * (2.0**-22)).astype(jnp.float8_e4m3fn).astype(F32)


def quantize(g):
    top = jnp.max(jnp.abs(g), axis=0, keepdims=True)
    scale = ((top + 1e-06) / 448.0).astype(BF16).astype(F32)
    return to_grid(g * (1.0 / scale)), scale


def encode(s):
    top = jnp.max(jnp.abs(s), axis=0, keepdims=True)
    norm = (top * 1.004 + 1e-30).astype(BF16)
    return jnp.exp2(s * (SPAN / norm.astype(F32))).astype(BF16), norm


def decode(code, norm):
    return jnp.log2(code.astype(F32)) * (norm * (1.0 / SPAN))


def rows_of(b):
    return pl.ds(b * BLOCK, BLOCK)


def lanes_of(q):
    return pl.ds(pl.multiple_of(q * PART, PART), PART)


HBM, VMEM = pltpu.MemorySpace.HBM, pltpu.MemorySpace.VMEM
ANY, WHOLE = pl.BlockSpec(memory_space=pl.ANY), pl.BlockSpec(memory_space=VMEM)
PARAMS = pltpu.CompilerParams(vmem_limit_bytes=24 * 2**20)


def near(*arrays):
    return [pltpu.with_memory_space_constraint(x, VMEM) for x in arrays]


def block_sum(local, b):
    total = None
    for i in range(local.shape[0]):
        codes, scale = quantize(local[i, rows_of(b), :])
        part = codes * scale
        total = part if total is None else total + part
    return total


def put_codes(out, start, totals):
    norms = []
    for b, total in enumerate(totals):
        code, norm = encode(total)
        out[pl.ds(start + b * BLOCK, BLOCK), :] = code
        norms.append(norm.astype(F32))
    return norms


def put_coded(out, totals):
    norms = put_codes(out, 0, totals)
    n = norms[0].shape[1]
    out[COLS : COLS + TAIL, :] = jnp.concatenate(
        norms + [jnp.zeros((TAIL - NBLK, n), F32)], axis=0
    ).astype(BF16)


def norms_of(ref, lanes):
    return ref[COLS : COLS + TAIL, lanes].astype(F32)


def get_coded(ref, lanes, norms, b):
    return decode(ref[rows_of(b), lanes], norms[b : b + 1, :])


def position():
    me = lax.axis_index("inner")
    return me // (2 * NX), (me // 2) % NX, me % 2


def part_for(k, q, other=False):
    y, x, c = position()
    c = 1 - c if other else c
    return 2 * jnp.where(c == 0, q * NX + (x + k) % NX, ((y + k) % NY) * NX + q) + c


SWAPPED = (1, 3, 0)


def send_kernel(a, g, *rest):
    outs, sems = rest[:3], rest[3:]
    parts = [
        [part_for(k, q, True) for k in SWAPPED for q in range(4)],
        [part_for(2, q) for q in range(4)],
        [part_for(2, q, True) for q in range(4)],
    ]
    copies = []
    for out, sem, group in zip(outs, sems, parts):
        n = len(group)
        for j, p in enumerate(group):
            copies.append(
                pltpu.make_async_copy(a.at[:, lanes_of(p)], out.at[:, pl.ds(j * PART, PART)], sem.at[j])
            )
        copies.append(pltpu.make_async_copy(g, out.at[:, pl.ds(n * PART, COLS)], sem.at[n]))
    for copy in copies:
        copy.start()
    for copy in copies:
        copy.wait()


def to_send(a, g):
    tok = a.shape[0]
    shapes = [(tok, 12 * PART + COLS)] + [(tok, 4 * PART + COLS)] * 2
    return pl.pallas_call(
        send_kernel,
        in_specs=[ANY, ANY],
        out_specs=[WHOLE] * 3,
        scratch_shapes=[pltpu.SemaphoreType.DMA((n,)) for n in (13, 5, 5)],
        out_shape=[pltpu.VMEM(shape, BF16) for shape in shapes],
        compiler_params=PARAMS,
    )(*[pltpu.with_memory_space_constraint(x, HBM) for x in (a, g)])


def sums_kernel(ks, kept, g_own, a_own, swapped, *rest):
    n = len(ks)
    far, outs, (abuf, gt, local, nbuf, asem) = rest[: 2 * kept], rest[2 * kept : 2 * kept + n], rest[2 * kept + n :]
    devices = 2 + len(far)

    def a_in(m, q):
        src = a_own.at[:, lanes_of(part_for(ks[m], q))]
        return pltpu.make_async_copy(src, abuf.at[4 * m + q], asem.at[4 * m + q])

    for j in range(4 * n):
        a_in(j // 4, j % 4).start()
    gt[0] = g_own[...].T
    gt[1] = swapped[:, 12 * PART :].T
    for i, other in enumerate(far):
        gt[2 + i] = other[:, 4 * PART :].T
    for m in range(n):

        def step(q, carry):
            lanes = lanes_of(q)
            a_in(m, q).wait()
            columns = [abuf[4 * m + q], swapped[:, lanes_of(4 * SWAPPED.index(ks[m]) + q)]]
            columns += [other[:, lanes] for other in far]
            for i in range(devices):
                local[i] = jnp.dot(gt[i], columns[i], preferred_element_type=F32)
            if kept:
                for b in range(NBLK):
                    outs[0][rows_of(b), lanes] = block_sum(local, b)
            else:
                start = pl.multiple_of(q * COLS, COLS)
                norms = put_codes(outs[m], start, [block_sum(local, b) for b in range(NBLK)])
                nbuf[q] = jnp.concatenate(norms, axis=0)
            return carry

        lax.fori_loop(0, 4, step, 0)
        if not kept:
            packed = jnp.concatenate([nbuf[q] for q in range(4)], axis=0)
            outs[m][4 * COLS :, :] = packed.astype(BF16)


def sums(ks, g_own, a_own, swapped, far=()):
    n, tok, kept = len(ks), a_own.shape[0], len(far) > 0
    devices = 2 + len(far)
    shape, dtype = ((COLS, 4 * PART), F32) if kept else ((4 * COLS + TAIL, PART), BF16)
    return pl.pallas_call(
        functools.partial(sums_kernel, ks, kept),
        in_specs=[WHOLE, ANY, WHOLE] + [WHOLE] * len(far),
        out_specs=[WHOLE] * n,
        scratch_shapes=[
            pltpu.VMEM((4 * n, tok, PART), BF16),
            pltpu.VMEM((devices, COLS, tok), BF16),
            pltpu.VMEM((devices, COLS, PART), F32),
            pltpu.VMEM((4, NBLK, PART), F32),
            pltpu.SemaphoreType.DMA((4 * n,)),
        ],
        out_shape=[pltpu.VMEM(shape, dtype)] * n,
        compiler_params=PARAMS,
        cost_estimate=pl.CostEstimate(
            flops=2 ** (36 if kept else 31), bytes_accessed=2**20, transcendentals=0
        ),
    )(*near(g_own), pltpu.with_memory_space_constraint(a_own, HBM), *near(swapped, *far))


def row_sum_kernel(own, r0, r1, out, nbuf):
    for i, r in enumerate((r0, r1)):
        norms = r[4 * COLS :, :].astype(F32)
        for q in range(4):
            nbuf[i, q] = norms[q * NBLK : (q + 1) * NBLK, :]

    def step(q, carry):
        lanes = lanes_of(q)
        start = pl.multiple_of(q * COLS, COLS)
        totals = []
        for b in range(NBLK):
            total = own[rows_of(b), lanes]
            for i, r in enumerate((r0, r1)):
                code = r[pl.ds(start + b * BLOCK, BLOCK), :]
                total = total + decode(code, nbuf[i, q, b : b + 1, :])
            totals.append(total)
        put_coded(out.at[q], totals)
        return carry

    lax.fori_loop(0, 4, step, 0)


def row_sum(own, r0, r1):
    return pl.pallas_call(
        row_sum_kernel,
        in_specs=[WHOLE] * 3,
        out_specs=WHOLE,
        out_shape=pltpu.VMEM((4, COLS + TAIL, PART), BF16),
        scratch_shapes=[pltpu.VMEM((2, 4, NBLK, PART), F32)],
        compiler_params=PARAMS,
    )(*near(own, r0, r1))


def group_kernel(got, out):
    n = got.shape[2]
    n_outer = out.shape[0]
    rows = n // n_outer
    lanes = slice(None)
    norms = [norms_of(got.at[s], lanes) for s in range(4)]
    for b in range(NBLK):
        total = get_coded(got.at[0], lanes, norms[0], b)
        for s in range(1, 4):
            total = total + get_coded(got.at[s], lanes, norms[s], b)
        codes, scale = quantize(total)
        sent = (codes * scale).T.astype(BF16)
        out[:, b * rows : (b + 1) * rows, :] = sent.reshape(n_outer, rows, BLOCK)


def group_sent(got, n_outer):
    return pl.pallas_call(
        group_kernel,
        in_specs=[WHOLE],
        out_specs=WHOLE,
        out_shape=pltpu.VMEM((n_outer, NBLK * (PART // n_outer), BLOCK), BF16),
        compiler_params=PARAMS,
    )(*near(got))


def final_kernel(got, out):
    rows = out.shape[0]
    for b in range(NBLK):
        total = jnp.zeros((rows, BLOCK), F32)
        for s in range(got.shape[0]):
            total = total + got[s, b * rows : (b + 1) * rows, :].astype(F32)
        out[:, b * BLOCK : (b + 1) * BLOCK] = total


def final_sum(got):
    rows = got.shape[1] // NBLK
    return pl.pallas_call(
        final_kernel,
        out_shape=jax.ShapeDtypeStruct((rows, COLS), F32),
        compiler_params=PARAMS,
    )(*near(got))


def index_of(y, x, c):
    return ((y % NY) * NX + x % NX) * 2 + c


def ring(k, cross=False):
    pairs = []
    for y in range(NY):
        for x in range(NX):
            pairs.append((index_of(y, x, int(cross)), index_of(y, x + k, 0)))
            pairs.append((index_of(y, x, 1 - int(cross)), index_of(y + k, x, 1)))
    return pairs


def columns():
    return [[index_of(y, x, 0) for y in range(NY)] for x in range(NX)] + [
        [index_of(y, x, 1) for x in range(NX)] for y in range(NY)
    ]


def shards(activations, output_grads):
    n_outer = lax.axis_size("outer")
    swap = [(i, i ^ 1) for i in range(2 * NX * NY)]
    to_swap, same, cross = to_send(activations, output_grads)
    swapped = lax.ppermute(to_swap, "inner", swap)
    far = (lax.ppermute(same, "inner", ring(2)), lax.ppermute(cross, "inner", ring(2, cross=True)))
    ahead, behind = sums((1, 3), output_grads, activations, swapped)
    got_ahead = lax.ppermute(ahead, "inner", ring(1))
    got_behind = lax.ppermute(behind, "inner", ring(3))
    (own,) = sums((0,), output_grads, activations, swapped, far)
    coded = row_sum(own, got_ahead, got_behind)
    got = lax.all_to_all(
        coded, "inner", split_axis=0, concat_axis=0, tiled=True, axis_index_groups=columns()
    )
    packed = group_sent(got, n_outer)
    return final_sum(lax.all_to_all(packed, "outer", split_axis=0, concat_axis=0, tiled=True))


def solution(mesh):
    return jax.shard_map(
        shards,
        mesh=mesh,
        in_specs=(P(("inner", "outer"), None), P(("inner", "outer"), None)),
        out_specs=P(("inner", "outer"), None),
        check_vma=False,
    )
```
